32 devices in a mesh: dp: 16 (over z, y, core), slab: 2 (over x).
Axes of the slice: x: 2, y: 2, z: 4, core: 2. Of those that a mesh axis runs over, the one named last changes fastest.
Arguments:
- snapshots: bfloat16 [16, 64, 512, 512], P('dp', None, 'slab'), may hold values from -6 to 6
- cotangent: bfloat16 [16, 64, 512, 512], P('dp', None, 'slab'), may hold values from -6 to 6
- w_spec: float32 [32, 32, 64, 128], P('slab', 'dp'), may hold values from -0.5 to 0.5
- first_moment: float32 [32, 32, 64, 128], P('slab', 'dp'), may hold values from -6 to 6
- second_moment: float32 [32, 32, 64, 128], P('slab', 'dp'), may hold values from 0.1 to 4
- w_skip: bfloat16 [64, 64], replicated, may hold values from -0.75 to 0.75
- bias: float32 [64], replicated, may hold values from -3 to 3
Outputs:
- layer_out: bfloat16 [16, 64, 512, 512], P('dp', None, 'slab')
- new_weights: float32 [32, 32, 64, 128], P('slab', 'dp')
- new_first: float32 [32, 32, 64, 128], P('slab', 'dp')
- new_second: float32 [32, 32, 64, 128], P('slab', 'dp')
The draws below stay inside these ranges and needn't reach their ends.
All inputs are finite; a program needn't handle non-finite values.
Results may differ from the reference program's by a relative error of at most 0.001.
Values sent between devices are 32-bit elements; how exact they have to be, the bound alone decides.
A program may use at most 192 MiB of HBM per device.

```python
import math
import jax
import jax.numpy as jnp
from jax import lax

C = 64
NY = 512
NZ = 512
KY = 32
KZ = 32
B = 16


def shard_levels(stream_key, dims, shards, least, high):
    loudness = 1.0
    for dim, parts in shards:
        heights = jax.random.uniform(jax.random.fold_in(jax.random.fold_in(stream_key, 6), dim), (parts,), jnp.float32, least / len(shards), high / len(shards))
        loudness = loudness * jnp.repeat(jnp.exp(heights), dims[dim] // parts).reshape((-1,) + (1,) * (len(dims) - 1 - dim))
    return loudness


def bell_draw(key, extent, scale, reach, pieces=(), held_as=jnp.bfloat16):
    result = scale * jax.random.normal(key, extent, jnp.float32)
    if pieces:
        result = result * shard_levels(key, extent, pieces, -0.22, 0.18)
    return jnp.clip(result, -reach, reach).astype(held_as)


def setup_inputs(seed: int = 0) -> dict:
    key_of = jax.random.split(jax.random.key(seed), 8)
    return {
        "snapshots": bell_draw(key_of[0], (B, C, NY, NZ), 1.0, 6.0, ((0, 16), (2, 2))),
        "cotangent": bell_draw(key_of[1], (B, C, NY, NZ), 1.0, 6.0, ((0, 16), (2, 2))),
        "w_spec": bell_draw(key_of[2], (KZ, KY, C, 2 * C), (2 * C) ** -0.5, 0.5, ((0, 2), (1, 16)), jnp.float32),
        "first_moment": bell_draw(key_of[3], (KZ, KY, C, 2 * C), 1.0, 6.0, ((0, 2), (1, 16)), jnp.float32),
        "second_moment": jnp.clip(jnp.exp(math.log(4.0) - 3.6888794 * jax.random.uniform(key_of[4], (KZ, KY, C, 2 * C), jnp.float32) ** shard_levels(key_of[4], (KZ, KY, C, 2 * C), ((0, 2), (1, 16)), -0.2, 0.2)), 0.1, 4.0),
        "w_skip": bell_draw(key_of[5], (C, C), C ** -0.5, 0.75),
        "bias": bell_draw(key_of[6], (C,), 0.5, 3.0, (), jnp.float32),
    }


high = lax.Precision.HIGHEST
gelu_coef = 0.7978845608028654
cube_coef = 0.044715

def gelu_value(x):
    return 0.5 * x * (1.0 + jnp.tanh(gelu_coef * (x + cube_coef * x * x * x)))

def gelu_slope(x):
    tanh_val = jnp.tanh(gelu_coef * (x + cube_coef * x * x * x))
    return 0.5 * (1.0 + tanh_val) + 0.5 * x * (1.0 - tanh_val * tanh_val) * gelu_coef * (1.0 + 3.0 * cube_coef * x * x)

def mode_index():
    half = KY // 2
    return jnp.concatenate([jnp.arange(half, dtype=jnp.int32), NY - half + jnp.arange(half, dtype=jnp.int32)])

def forward_modes(field):
    along_z = jnp.fft.rfft(field, axis=2)[:, :, :KZ]
    both = jnp.fft.fft(along_z, axis=1)
    picked = jnp.take(both, mode_index(), axis=1)
    return (jnp.real(picked), jnp.imag(picked))

def inverse_modes(real_part, imag_part):
    index = mode_index()
    full_real = jnp.zeros((C, NY, NZ), jnp.float32).at[:, index, :KZ].set(real_part)
    full_imag = jnp.zeros((C, NY, NZ), jnp.float32).at[:, index, :KZ].set(imag_part)
    spectrum = lax.complex(full_real, -full_imag)
    return jnp.real(jnp.fft.fft2(spectrum, axes=(1, 2)))

def reference(snapshots, cotangent, w_spec, first_moment, second_moment, w_skip, bias):
    count = snapshots.shape[0]
    w_real = w_spec[..., :C]
    w_imag = w_spec[..., C:]
    spec_scale = 1.0 / math.sqrt(NY * NZ)
    out_scale = 1.0 / math.sqrt(KY * KZ)
    skip_weight = w_skip.astype(jnp.float32)

    def one(total, inputs):
        field_low, cot_low = inputs
        field = field_low.astype(jnp.float32)
        ur, ui = forward_modes(field)
        ur = ur * spec_scale
        ui = ui * spec_scale
        vr = jnp.einsum('ijk,kjio->ojk', ur, w_real, precision=high) - jnp.einsum('ijk,kjio->ojk', ui, w_imag, precision=high)
        vi = jnp.einsum('ijk,kjio->ojk', ur, w_imag, precision=high) + jnp.einsum('ijk,kjio->ojk', ui, w_real, precision=high)
        mixed = inverse_modes(vr, vi) * out_scale
        skip = jnp.einsum('io,iyz->oyz', skip_weight, field, precision=high)
        pre = mixed + skip + bias[:, None, None]
        out = gelu_value(pre).astype(jnp.bfloat16)
        slope = cot_low.astype(jnp.float32) * gelu_slope(pre)
        gr, gi = forward_modes(slope)
        gr = gr * out_scale
        gi = gi * out_scale
        grad_real = jnp.einsum('ijk,ojk->kjio', ur, gr, precision=high) + jnp.einsum('ijk,ojk->kjio', ui, gi, precision=high)
        grad_imag = jnp.einsum('ijk,ojk->kjio', ur, gi, precision=high) - jnp.einsum('ijk,ojk->kjio', ui, gr, precision=high)
        return (total + jnp.concatenate([grad_real, grad_imag], axis=-1), out)
    init = jnp.zeros(w_spec.shape, jnp.float32)
    total, outs = lax.scan(one, init, (snapshots, cotangent))
    grad = total / count
    new_first = 0.9 * first_moment + 0.1 * grad
    new_second = 0.95 * second_moment + 0.05 * grad * grad
    bias_first = 1.0 - 0.9 ** 10
    bias_second = 1.0 - 0.95 ** 10
    new_weights = w_spec - 0.01 * (new_first / bias_first) / (jnp.sqrt(new_second / bias_second) + 1e-08)
    return (outs, new_weights, new_first, new_second)
```

```python
import functools
import math

import jax
import jax.numpy as jnp
import ml_dtypes
import numpy as np
from jax import lax
from jax.experimental import pallas as pl
from jax.experimental.pallas import tpu as pltpu
from jax.sharding import PartitionSpec as P

NY = 512
NZ = 512
KY = 32
KZ = 32
ROWS = 16

high = lax.Precision.HIGHEST
gelu_coef = 0.7978845608028654
cube_coef = 0.044715
vmem_bytes = 56 * 1024 * 1024


def halves(table):
    top = table.astype(ml_dtypes.bfloat16)
    rest = (table - top.astype(np.float64)).astype(ml_dtypes.bfloat16)
    return top, rest


def z_table():
    angle = 2.0 * math.pi / NZ * (np.outer(np.arange(NZ), np.arange(KZ)) % NZ)
    return np.concatenate([np.cos(angle), -np.sin(angle)], 1)


def y_table():
    freq = np.concatenate([np.arange(KY // 2), np.arange(KY // 2) - KY // 2])
    angle = 2.0 * math.pi / NY * (np.outer(np.arange(NY), freq) % NY)
    return np.concatenate([np.cos(angle), np.sin(angle)], 1)


def split(x):
    top = x.astype(jnp.bfloat16)
    return top, (x - top.astype(jnp.float32)).astype(jnp.bfloat16)


def mm(a, b):
    return jnp.dot(a, b, preferred_element_type=jnp.float32)


def y_modes(zval, ytab):
    top, rest = split(zval)
    both = mm(ytab, top)
    w = both[: 2 * KY] + both[2 * KY :] + mm(ytab[: 2 * KY], rest)
    real = w[:KY, :KZ] + w[KY:, KZ:]
    imag = w[:KY, KZ:] - w[KY:, :KZ]
    return jnp.concatenate([real, imag], axis=1)


def forward_kernel(x_ref, zt_ref, yt_ref, o_ref):
    for c in range(x_ref.shape[0]):
        zval = mm(x_ref[c], zt_ref[...])
        o_ref[c] = y_modes(zval[:, : 2 * KZ] + zval[:, 2 * KZ :], yt_ref[...])


def point_kernel(
    x_ref, cot_ref, spec_ref, bias_ref, kron_ref, zt_ref, yt_ref, back_ref, yback_ref,
    out_ref, g_ref, left, zsum,
):
    step = pl.program_id(0)
    chans, rows = left.shape[:2]
    wide = 2 * KZ

    @pl.when(step == 0)
    def _():
        @pl.loop(0, chans)
        def _(o):
            v = spec_ref[o]
            turned = jnp.concatenate([-v[:, KZ:], v[:, :KZ]], axis=1)
            top, rest = split(jnp.concatenate([v, turned], axis=0))
            yval = mm(yback_ref[...], jnp.concatenate([top, rest, top], axis=0))
            ytop, yrest = split(yval)
            b = bias_ref[o]
            b0 = b.astype(jnp.bfloat16).astype(jnp.float32)
            b1 = (b - b0).astype(jnp.bfloat16).astype(jnp.float32)
            lane = lax.broadcasted_iota(jnp.int32, b.shape, 1)
            terms = jnp.where(lane == 0, b0, jnp.where(lane == 1, b1, b - b0 - b1))
            terms = jnp.broadcast_to(terms, (rows, wide)).astype(jnp.bfloat16)
            left[o] = jnp.concatenate([ytop, yrest, ytop, terms], axis=1)

    here = pl.ds(pl.multiple_of(step * ROWS, ROWS), ROWS)
    x = x_ref[...].reshape(chans * ROWS, NZ)
    part = chans // 2
    for m in range(2):
        own = slice(m * part, (m + 1) * part)
        pre = mm(kron_ref[m * part * ROWS : (m + 1) * part * ROWS, :], x)
        pre += mm(left[own, here, :].reshape(part * ROWS, 4 * wide), back_ref[...])
        sq = pre * pre
        t = jnp.tanh(pre * (gelu_coef + (gelu_coef * cube_coef) * sq))
        h = 0.5 + 0.5 * t
        value = pre * h
        out_ref[own] = value.astype(jnp.bfloat16).reshape(part, ROWS, NZ)
        grow = 2.0 * gelu_coef + (6.0 * gelu_coef * cube_coef) * sq
        cot = cot_ref[own].reshape(part * ROWS, NZ).astype(jnp.float32)
        slope = cot * (h + value * (0.5 - 0.5 * t) * grow)
        top, rest = split(slope)
        zval = mm(top, zt_ref[...])
        zval = zval[:, :wide] + zval[:, wide:] + mm(rest, zt_ref[:, :wide])
        zsum[own, here, :] = zval.reshape(part, ROWS, wide)

    @pl.when(step == pl.num_programs(0) - 1)
    def _():
        @pl.loop(0, chans)
        def _(o):
            g_ref[o] = y_modes(zsum[o], yt_ref[...])


def whole(shape):
    return pl.BlockSpec(shape, lambda i: (0,) * len(shape))


def forward_modes(field, zt, yt):
    chans, rows, length = field.shape
    per = 8
    return pl.pallas_call(
        forward_kernel,
        grid=(chans // per,),
        in_specs=[
            pl.BlockSpec((per, rows, length), lambda i: (i, 0, 0)),
            whole(zt.shape),
            whole(yt.shape),
        ],
        out_specs=pl.BlockSpec((per, KY, 2 * KZ), lambda i: (i, 0, 0)),
        out_shape=jax.ShapeDtypeStruct((chans, KY, 2 * KZ), jnp.float32),
        compiler_params=pltpu.CompilerParams(vmem_limit_bytes=vmem_bytes),
    )(field, zt, yt)


def point_part(field, cot, spec, bias, kron, zt, yt, back, yback):
    chans, rows, length = field.shape
    rowed = pl.BlockSpec((chans, ROWS, length), lambda i: (0, i, 0))
    return pl.pallas_call(
        point_kernel,
        grid=(rows // ROWS,),
        in_specs=[rowed, rowed]
        + [whole(a.shape) for a in (spec, bias, kron, zt, yt, back, yback)],
        out_specs=[rowed, whole((chans, KY, 2 * KZ))],
        out_shape=[
            jax.ShapeDtypeStruct(field.shape, jnp.bfloat16),
            jax.ShapeDtypeStruct((chans, KY, 2 * KZ), jnp.float32),
        ],
        scratch_shapes=[
            pltpu.VMEM((chans, rows, 8 * KZ), jnp.bfloat16),
            pltpu.VMEM((chans, rows, 2 * KZ), jnp.float32),
        ],
        compiler_params=pltpu.CompilerParams(vmem_limit_bytes=vmem_bytes),
    )(field, cot, spec, bias, kron, zt, yt, back, yback)


def to_owner(modes, dp, slab):
    chans = modes.shape[0]
    x = modes.reshape(chans, dp, KY // dp, 2, slab, KZ // slab)
    x = x.transpose(1, 4, 5, 2, 3, 0).reshape(dp * slab, -1, chans)
    x = lax.all_to_all(x, ("dp", "slab"), split_axis=0, concat_axis=0, tiled=True)
    x = x.reshape(dp, slab, KZ // slab, KY // dp, 2, chans).sum(1)
    return x.transpose(1, 2, 0, 3, 4)


def from_owner(spec, dp, slab):
    chans = spec.shape[-1]
    x = spec.transpose(2, 0, 1, 3, 4).reshape(dp, 1, -1, chans)
    x = jnp.broadcast_to(x, (dp, slab) + x.shape[2:]).reshape(dp * slab, -1, chans)
    x = lax.all_to_all(x, ("dp", "slab"), split_axis=0, concat_axis=0, tiled=True)
    x = x.reshape(dp, slab, KZ // slab, KY // dp, 2, chans)
    return x.transpose(5, 0, 3, 4, 1, 2).reshape(chans, KY, 2 * KZ)


def body(snapshots, cotangent, w_spec, first_moment, second_moment, w_skip, bias):
    chans, rows, length = snapshots.shape[1:]
    spec_scale = 1.0 / math.sqrt(NY * NZ)
    out_scale = 1.0 / math.sqrt(KY * KZ)
    dp = lax.axis_size("dp")
    slab = lax.axis_size("slab")
    start = lax.axis_index("slab") * rows
    ztop, zrest = halves(z_table())
    ytop, yrest = halves(y_table())
    zt = jnp.asarray(np.concatenate([ztop, zrest], 1))
    ones = np.zeros((2 * KZ, length), ml_dtypes.bfloat16)
    ones[:3] = 1
    back = jnp.asarray(np.concatenate([ztop.T, ztop.T, zrest.T, ones], 0))
    yt = jnp.asarray(np.concatenate([ytop, yrest], 1).T)
    yt = lax.dynamic_slice_in_dim(yt, start, rows, 1)
    yback = jnp.asarray(np.concatenate([ytop, ytop, yrest], 1))
    yback = lax.dynamic_slice_in_dim(yback, start, rows, 0)
    same = jnp.eye(ROWS, dtype=jnp.bfloat16)
    kron = w_skip.T[:, None, :, None] * same[None, :, None, :]
    kron = kron.reshape(chans * ROWS, chans * ROWS)
    bias_lanes = jnp.pad(
        jnp.broadcast_to(bias[:, None, None], (chans, 1, 3)), ((0, 0), (0, 0), (0, 2 * KZ - 3))
    )

    u = to_owner(forward_modes(snapshots[0], zt, yt), dp, slab) * spec_scale
    prod = jnp.einsum("kjbri,kjio->kjbro", u, w_spec, precision=high)
    vreal = prod[..., 0, :chans] - prod[..., 1, chans:]
    vimag = prod[..., 0, chans:] + prod[..., 1, :chans]
    spec = from_owner(jnp.stack([vreal, vimag], 3) * out_scale, dp, slab)
    layer_out, gmodes = point_part(
        snapshots[0], cotangent[0], spec, bias_lanes, kron, zt, yt, back, yback
    )
    g = to_owner(gmodes, dp, slab) * (out_scale / dp)
    turned = jnp.stack([g[..., 1, :], -g[..., 0, :]], 3)
    pair = jnp.concatenate([g, turned], -1)
    grad = jnp.einsum("kjbri,kjbro->kjio", u, pair, precision=high)
    new_first = 0.9 * first_moment + 0.1 * grad
    new_second = 0.95 * second_moment + 0.05 * grad * grad
    bias_first = 1.0 - 0.9**10
    bias_second = 1.0 - 0.95**10
    new_weights = w_spec - 0.01 * (new_first / bias_first) / (
        jnp.sqrt(new_second / bias_second) + 1e-08
    )
    return (layer_out[None], new_weights, new_first, new_second)


def solution(mesh):
    placed = (
        P("dp", None, "slab", None),
        P("dp", None, "slab", None),
        P("slab", "dp", None, None),
        P("slab", "dp", None, None),
        P("slab", "dp", None, None),
        P(),
        P(),
    )
    return jax.shard_map(
        body,
        mesh=mesh,
        in_specs=placed,
        out_specs=(
            P("dp", None, "slab", None),
            P("slab", "dp", None, None),
            P("slab", "dp", None, None),
            P("slab", "dp", None, None),
        ),
        check_vma=False,
    )
```

```python
import functools
import math

import jax
import jax.numpy as jnp
import ml_dtypes
import numpy as np
from jax import lax
from jax.experimental import pallas as pl
from jax.experimental.pallas import tpu as pltpu
from jax.sharding import PartitionSpec as P

NY = 512
NZ = 512
KY = 32
KZ = 32
ROWS = 16
SUB = 8

high = lax.Precision.HIGHEST
gelu_coef = 0.7978845608028654
cube_coef = 0.044715
vmem_bytes = 56 * 1024 * 1024


def halves(table):
    top = table.astype(ml_dtypes.bfloat16)
    rest = (table - top.astype(np.float64)).astype(ml_dtypes.bfloat16)
    return top, rest


def z_table():
    angle = 2.0 * math.pi / NZ * (np.outer(np.arange(NZ), np.arange(KZ)) % NZ)
    return np.concatenate([np.cos(angle), -np.sin(angle)], 1)


def y_table():
    freq = np.concatenate([np.arange(KY // 2), np.arange(KY // 2) - KY // 2])
    angle = 2.0 * math.pi / NY * (np.outer(np.arange(NY), freq) % NY)
    return np.concatenate([np.cos(angle), np.sin(angle)], 1)


def split(x):
    top = x.astype(jnp.bfloat16)
    return top, (x - top.astype(jnp.float32)).astype(jnp.bfloat16)


def mm(a, b):
    return jnp.dot(a, b, preferred_element_type=jnp.float32)


def one_hot(shape, test):
    rows = lax.broadcasted_iota(jnp.int32, shape, 0)
    columns = lax.broadcasted_iota(jnp.int32, shape, 1)
    return jnp.where(test(rows, columns), 1.0, 0.0).astype(jnp.bfloat16)


def each(count, step):
    per = 8

    @pl.loop(0, count // per)
    def _(i):
        for n in range(per):
            step(i * per + n)


def y_modes(zval, ytab):
    top, rest = split(zval)
    both = mm(ytab, jnp.concatenate([top, rest], axis=1))
    first = both[: 2 * KY]
    w = first[:, : 2 * KZ] + first[:, 2 * KZ :] + both[2 * KY :, : 2 * KZ]
    real = w[:KY, :KZ] + w[KY:, KZ:]
    imag = w[:KY, KZ:] - w[KY:, :KZ]
    return jnp.concatenate([real, imag], axis=1)


def forward_kernel(x_ref, zt_ref, yt_ref, o_ref):
    per, rows, length = x_ref.shape
    zval = mm(x_ref[...].reshape(per * rows, length), zt_ref[...])
    zval = (zval[:, : 2 * KZ] + zval[:, 2 * KZ :]).reshape(per, rows, 2 * KZ)
    for c in range(per):
        o_ref[c] = y_modes(zval[c], yt_ref[...])


def point_kernel(
    x_ref, cot_ref, spec_ref, bias_ref, skip_ref, zt_ref, yt_ref, back_ref, yback_ref,
    out_ref, g_ref, left, zsum, kron_ref,
):
    step = pl.program_id(0)
    chans, rows = left.shape[:2]
    wide = 2 * KZ

    @pl.when(step == 0)
    def _():
        tall = chans * SUB
        part = tall // 4
        spread = one_hot((chans, tall), lambda i, r: i == r // SUB)
        for m in range(4):
            pick = one_hot((part, chans), lambda r, o: (r + m * part) // SUB == o)
            rows_of = mm(pick, skip_ref[...]).astype(jnp.bfloat16)
            same = one_hot((part, tall), lambda r, s: r % SUB == s % SUB)
            kron_ref[m * part : (m + 1) * part, :] = (
                mm(rows_of, spread).astype(jnp.bfloat16) * same
            )

        def invert(o):
            v = spec_ref[o]
            turned = jnp.concatenate([-v[:, KZ:], v[:, :KZ]], axis=1)
            top, rest = split(jnp.concatenate([v, turned], axis=0))
            yval = mm(yback_ref[...], jnp.concatenate([top, rest, top], axis=0))
            ytop, yrest = split(yval)
            b = bias_ref[o]
            b0 = b.astype(jnp.bfloat16).astype(jnp.float32)
            b1 = (b - b0).astype(jnp.bfloat16).astype(jnp.float32)
            lane = lax.broadcasted_iota(jnp.int32, b.shape, 1)
            terms = jnp.where(lane == 0, b0, jnp.where(lane == 1, b1, b - b0 - b1))
            terms = jnp.broadcast_to(terms, (rows, wide)).astype(jnp.bfloat16)
            left[o] = jnp.concatenate([ytop, yrest, ytop, terms], axis=1)

        each(chans, invert)

    here = pl.ds(pl.multiple_of(step * ROWS, ROWS), ROWS)
    field = x_ref[...].astype(jnp.float32)
    terms = left[:, here, :].astype(jnp.float32)
    values = []
    for m in range(ROWS // SUB):
        own = slice(m * SUB, (m + 1) * SUB)
        x = field[:, own].reshape(chans * SUB, NZ).astype(jnp.bfloat16)
        term = terms[:, own].reshape(chans * SUB, 4 * wide).astype(jnp.bfloat16)
        pre = mm(kron_ref[...], x) + mm(term, back_ref[...])
        sq = pre * pre
        t = jnp.tanh(pre * (gelu_coef + (gelu_coef * cube_coef) * sq))
        h = 0.5 + 0.5 * t
        value = pre * h
        values.append(value.reshape(chans, SUB, NZ))
        grow = 2.0 * gelu_coef + (6.0 * gelu_coef * cube_coef) * sq
        cot = cot_ref[...].astype(jnp.float32)[:, own].reshape(chans * SUB, NZ)
        slope = cot * (h + value * (0.5 - 0.5 * t) * grow)
        top, rest = split(slope)
        zval = mm(top, zt_ref[...])
        zval = zval[:, :wide] + zval[:, wide:] + mm(rest, zt_ref[:, :wide])
        place = pl.ds(pl.multiple_of(step * ROWS + m * SUB, SUB), SUB)
        zsum[:, place, :] = zval.reshape(chans, SUB, wide)
    out_ref[...] = jnp.concatenate(values, axis=1).astype(jnp.bfloat16)

    @pl.when(step == pl.num_programs(0) - 1)
    def _():
        def forward(o):
            g_ref[o] = y_modes(zsum[o], yt_ref[...])

        each(chans, forward)


def whole(shape):
    return pl.BlockSpec(shape, lambda i: (0,) * len(shape))


def forward_modes(field, zt, yt):
    chans, rows, length = field.shape
    per = 8
    return pl.pallas_call(
        forward_kernel,
        grid=(chans // per,),
        in_specs=[
            pl.BlockSpec((per, rows, length), lambda i: (i, 0, 0)),
            whole(zt.shape),
            whole(yt.shape),
        ],
        out_specs=pl.BlockSpec((per, KY, 2 * KZ), lambda i: (i, 0, 0)),
        out_shape=jax.ShapeDtypeStruct((chans, KY, 2 * KZ), jnp.float32),
        compiler_params=pltpu.CompilerParams(vmem_limit_bytes=vmem_bytes),
    )(field, zt, yt)


def point_part(field, cot, spec, bias, skip, zt, yt, back, yback):
    chans, rows, length = field.shape
    rowed = pl.BlockSpec((chans, ROWS, length), lambda i: (0, i, 0))
    return pl.pallas_call(
        point_kernel,
        grid=(rows // ROWS,),
        in_specs=[rowed, rowed]
        + [whole(a.shape) for a in (spec, bias, skip, zt, yt, back, yback)],
        out_specs=[rowed, whole((chans, KY, 2 * KZ))],
        out_shape=[
            jax.ShapeDtypeStruct(field.shape, jnp.bfloat16),
            jax.ShapeDtypeStruct((chans, KY, 2 * KZ), jnp.float32),
        ],
        scratch_shapes=[
            pltpu.VMEM((chans, rows, 8 * KZ), jnp.bfloat16),
            pltpu.VMEM((chans, rows, 2 * KZ), jnp.float32),
            pltpu.VMEM((chans * SUB, chans * SUB), jnp.bfloat16),
        ],
        compiler_params=pltpu.CompilerParams(vmem_limit_bytes=vmem_bytes),
    )(field, cot, spec, bias, skip, zt, yt, back, yback)


def to_owner(modes, dp, slab):
    chans = modes.shape[0]
    x = modes.reshape(chans, dp, KY // dp, 2, slab, KZ // slab)
    x = x.transpose(1, 4, 5, 2, 3, 0).reshape(dp * slab, -1, chans)
    x = lax.all_to_all(x, ("dp", "slab"), split_axis=0, concat_axis=0, tiled=True)
    x = x.reshape(dp, slab, KZ // slab, KY // dp, 2, chans).sum(1)
    return x.transpose(1, 2, 0, 3, 4)


def from_owner(spec, dp, slab):
    chans = spec.shape[-1]
    x = spec.transpose(2, 0, 1, 3, 4).reshape(dp, 1, -1, chans)
    x = jnp.broadcast_to(x, (dp, slab) + x.shape[2:]).reshape(dp * slab, -1, chans)
    x = lax.all_to_all(x, ("dp", "slab"), split_axis=0, concat_axis=0, tiled=True)
    x = x.reshape(dp, slab, KZ // slab, KY // dp, 2, chans)
    return x.transpose(5, 0, 3, 4, 1, 2).reshape(chans, KY, 2 * KZ)


def body(snapshots, cotangent, w_spec, first_moment, second_moment, w_skip, bias):
    chans, rows, length = snapshots.shape[1:]
    spec_scale = 1.0 / math.sqrt(NY * NZ)
    out_scale = 1.0 / math.sqrt(KY * KZ)
    dp = lax.axis_size("dp")
    slab = lax.axis_size("slab")
    start = lax.axis_index("slab") * rows
    ztop, zrest = halves(z_table())
    ytop, yrest = halves(y_table())
    zt = jnp.asarray(np.concatenate([ztop, zrest], 1))
    ones = np.zeros((2 * KZ, length), ml_dtypes.bfloat16)
    ones[:3] = 1
    back = jnp.asarray(np.concatenate([ztop.T, ztop.T, zrest.T, ones], 0))
    yt = jnp.asarray(np.concatenate([ytop, yrest], 1).T)
    yt = lax.dynamic_slice_in_dim(yt, start, rows, 1)
    yback = jnp.asarray(np.concatenate([ytop, ytop, yrest], 1))
    yback = lax.dynamic_slice_in_dim(yback, start, rows, 0)
    bias_lanes = jnp.pad(
        jnp.broadcast_to(bias[:, None, None], (chans, 1, 3)), ((0, 0), (0, 0), (0, 2 * KZ - 3))
    )

    u = to_owner(forward_modes(snapshots[0], zt, yt), dp, slab) * spec_scale
    prod = jnp.einsum("kjbri,kjio->kjbro", u, w_spec, precision=high)
    vreal = prod[..., 0, :chans] - prod[..., 1, chans:]
    vimag = prod[..., 0, chans:] + prod[..., 1, :chans]
    spec = from_owner(jnp.stack([vreal, vimag], 3) * out_scale, dp, slab)
    layer_out, gmodes = point_part(
        snapshots[0], cotangent[0], spec, bias_lanes, w_skip.T, zt, yt, back, yback
    )
    g = to_owner(gmodes, dp, slab) * (out_scale / dp)
    turned = jnp.stack([g[..., 1, :], -g[..., 0, :]], 3)
    pair = jnp.concatenate([g, turned], -1)
    grad = jnp.einsum("kjbri,kjbro->kjio", u, pair, precision=high)
    new_first = 0.9 * first_moment + 0.1 * grad
    new_second = 0.95 * second_moment + 0.05 * grad * grad
    bias_first = 1.0 - 0.9**10
    bias_second = 1.0 - 0.95**10
    new_weights = w_spec - 0.01 * (new_first / bias_first) / (
        jnp.sqrt(new_second / bias_second) + 1e-08
    )
    return (layer_out[None], new_weights, new_first, new_second)


def solution(mesh):
    placed = (
        P("dp", None, "slab", None),
        P("dp", None, "slab", None),
        P("slab", "dp", None, None),
        P("slab", "dp", None, None),
        P("slab", "dp", None, None),
        P(),
        P(),
    )
    return jax.shard_map(
        body,
        mesh=mesh,
        in_specs=placed,
        out_specs=(
            P("dp", None, "slab", None),
            P("slab", "dp", None, None),
            P("slab", "dp", None, None),
            P("slab", "dp", None, None),
        ),
        check_vma=False,
    )
```
